32 devices in a mesh: groups: 2 (over x), rows: 16 (over z, y, core).
Axes of the slice: x: 2, y: 2, z: 4, core: 2. Of those that a mesh axis runs over, the one named last changes fastest.
Arguments:
- tracer: float32 [128, 16384], P('groups', 'rows'), parts along dimension 0, may hold values from -6 to 6
- source: float32 [128, 16384], P('groups', 'rows'), parts along dimension 0, may hold values from -6 to 6
- exp_month_a: bfloat16 [128, 8, 128, 128], P('rows'), may hold values from -0.1875 to 0.1875
- exp_month_b: bfloat16 [128, 8, 128, 128], P('rows'), may hold values from -0.1875 to 0.1875
- imp_month_a: bfloat16 [128, 8, 128, 128], P('rows'), may hold values from -0.1875 to 0.1875
- imp_month_b: bfloat16 [128, 8, 128, 128], P('rows'), may hold values from -0.1875 to 0.1875
- col_index: int32 [128, 8], P('rows'), may hold values from 0 to 11, as said below
- block_count: int32 [128], P('rows'), may hold values from 2 to 8
- send_list: int32 [16, 4, 1], P('rows'), may hold values from 0 to 7, as said below
- wet_rows: int32 [128], P('rows'), may hold values from 32 to 128
- month_day: int32 [2], replicated, may hold values from 0 to 30
Outputs:
- tracer_out: float32 [128, 16384], P('groups', 'rows'), parts along dimension 0
The draws below stay inside these ranges and needn't reach their ends.
There are 2 independent parts, one for each index of `groups`. The reference program is written for one: setup_inputs(seed, part) draws one part's arguments, and reference() takes and returns one part's arrays. A program takes and returns all parts, laid end to end along the dimension named above; an argument that names none is the same for every part. Nothing has to cross between parts.
Inputs may be any that keep to these rules, and one draw needn't show every extreme that they name: `col_index`: slot 0 of row block r is its own local block r % 8; no slot names a device outside the curve. `send_list`: the 1 entries of one device and direction are distinct.
All inputs are finite; a program needn't handle non-finite values.
Results may differ from the reference program's by a relative error of at most 0.0047.
Values may be sent and summed in bfloat16 or wider, within the bound.
No kernel may reach another device: no remote copies, remote signals or barrier semaphores. Data moves between devices by JAX's collectives and lax.ppermute only.
A program may use at most 64 MiB of HBM per device.

```python
import jax
import jax.numpy as jnp
from jax import lax

TRACERS = 64
BLK = 128
RB = 8
K = 8
HALO = 1
STEPS = 2
DAYS = 30
STRIDE = 4
NBLK = 128


def draw_col_index(key, part):
    key = jax.random.fold_in(key, 11)
    slot_total = RB + 4 * HALO
    picks = jax.random.randint(key, (NBLK, K), 0, slot_total)
    owner = jnp.arange(NBLK) // RB
    device_total = NBLK // RB
    offsets = jnp.array([1, -1, STRIDE, -STRIDE], jnp.int32)
    direction = jnp.clip((picks - RB) // HALO, 0, 3)
    sender = owner[:, None] - offsets[direction]
    usable = (picks < RB) | (sender >= 0) & (sender < device_total)
    picks = jnp.where(usable, picks, picks % RB)
    picks = picks.at[:, 0].set(jnp.arange(NBLK) % RB)
    return picks.astype(jnp.int32)


def draw_block_count(key, part):
    key = jax.random.fold_in(key, 12)
    first_key, second_key, third_key = jax.random.split(key, 3)
    counts = jax.random.randint(first_key, (NBLK,), 2, K + 1)
    top_place = jax.random.randint(second_key, (), 0, NBLK)
    low_place = (top_place + 1 + jax.random.randint(third_key, (), 0, NBLK - 1)) % NBLK
    counts = counts.at[top_place].set(K).at[low_place].set(2)
    return counts.astype(jnp.int32)


def draw_send_list(key, part):
    key = jax.random.fold_in(key, 13)
    scores = jax.random.randint(key, (NBLK // RB, 4, RB), 0, 1 << 20) * RB + jnp.arange(RB)
    return jnp.argsort(scores, axis=-1)[..., :HALO].astype(jnp.int32)


def draw_wet_rows(key, part):
    key = jax.random.fold_in(key, 14)
    first_key, second_key, third_key = jax.random.split(key, 3)
    counts = jax.random.randint(first_key, (NBLK,), BLK // 4, BLK + 1)
    top_place = jax.random.randint(second_key, (), 0, NBLK)
    low_place = (top_place + 1 + jax.random.randint(third_key, (), 0, NBLK - 1)) % NBLK
    counts = counts.at[top_place].set(BLK).at[low_place].set(BLK // 4)
    return counts.astype(jnp.int32)


def block_scale(key, shape, cuts, low, high):
    def one(position, parts):
        draws = jax.random.uniform(jax.random.fold_in(jax.random.fold_in(key, 6), position), (parts,), jnp.float32, low / len(cuts), high / len(cuts))
        return jnp.repeat(jnp.exp(draws), shape[position] // parts).reshape((-1,) + (1,) * (len(shape) - position - 1))

    factor_of = one(*cuts[0])
    for cut in cuts[1:]:
        factor_of = factor_of * one(*cut)
    return factor_of


def bell_draw(stream_key, dims, spread, limit, cuts=(), held_as=jnp.bfloat16):
    result = jax.random.normal(stream_key, dims, jnp.float32) * spread
    if len(cuts) > 0:
        result = block_scale(stream_key, dims, cuts, -0.22, 0.18) * result
    return jnp.clip(result, min=-limit, max=limit).astype(held_as)


def setup_inputs(seed: int = 0, part: int = 0) -> dict:
    key_list = jax.random.split(jax.random.key(seed), 12)
    own_keys = jax.random.split(jax.random.fold_in(key_list[11], part), 12)
    return {
        "tracer": bell_draw(own_keys[0], (TRACERS, NBLK * BLK), 1.0, 6.0, ((1, 16),), jnp.float32),
        "source": bell_draw(own_keys[1], (TRACERS, NBLK * BLK), 1.0, 6.0, ((1, 16),), jnp.float32),
        "exp_month_a": bell_draw(key_list[2], (NBLK, K, BLK, BLK), (K * BLK) ** -0.5, 0.1875, ((0, 16),)),
        "exp_month_b": bell_draw(key_list[3], (NBLK, K, BLK, BLK), (K * BLK) ** -0.5, 0.1875, ((0, 16),)),
        "imp_month_a": bell_draw(key_list[4], (NBLK, K, BLK, BLK), (K * BLK) ** -0.5, 0.1875, ((0, 16),)),
        "imp_month_b": bell_draw(key_list[5], (NBLK, K, BLK, BLK), (K * BLK) ** -0.5, 0.1875, ((0, 16),)),
        "col_index": draw_col_index(jax.random.fold_in(key_list[11], 71), part),
        "block_count": draw_block_count(jax.random.fold_in(key_list[11], 71), part),
        "send_list": draw_send_list(jax.random.fold_in(key_list[11], 71), part),
        "wet_rows": draw_wet_rows(jax.random.fold_in(key_list[11], 71), part),
        "month_day": jax.random.randint(key_list[10], (STEPS,), 0, DAYS + 1).astype(jnp.int32),
    }


def blend_months(month_first, month_second, month_now):
    late_weight = month_now.astype(jnp.float32)
    early_weight = (DAYS - month_now).astype(jnp.float32)
    mixed = early_weight * month_first.astype(jnp.float32) + late_weight * month_second.astype(jnp.float32)
    return (mixed / DAYS).astype(jnp.bfloat16)


def from_device(blocks, offset):
    device_total = blocks.shape[0]
    zero_rows = jnp.zeros((abs(offset),) + blocks.shape[1:], blocks.dtype)
    if offset > 0:
        return jnp.concatenate([zero_rows, blocks[:device_total - offset]], 0)
    return jnp.concatenate([blocks[-offset:], zero_rows], 0)


def extend_blocks(rounded, send_list):
    device_total = rounded.shape[0]
    outgoing = jax.vmap(lambda own_blocks, chosen_rows: own_blocks[:, chosen_rows.reshape(-1), :])(rounded, send_list)
    outgoing = outgoing.reshape(device_total, rounded.shape[1], 4, HALO, BLK)
    offsets = (1, -1, STRIDE, -STRIDE)
    incoming = [from_device(outgoing[:, :, direction], offsets[direction]) for direction in range(4)]
    return jnp.concatenate([rounded] + incoming, 2)


def apply_blocks(extended, columns, slot_mask, month_first, month_second, month_now):
    def one_device(pieces):
        blocks, column_part, mask_part, first_part, second_part = pieces
        matrix = blend_months(first_part, second_part, month_now)
        picked = blocks[:, column_part, :] * mask_part[None, :, :, None]
        return jnp.einsum("trkj,rkij->tri", picked.astype(jnp.float32), matrix.astype(jnp.float32))
    return lax.map(one_device, (extended, columns, slot_mask, month_first, month_second))


def reference(tracer, source, exp_month_a, exp_month_b, imp_month_a, imp_month_b, col_index, block_count, send_list, wet_rows, month_day):
    device_total = NBLK // RB

    def by_device(field):
        return field.reshape(TRACERS, device_total, RB, BLK).transpose(1, 0, 2, 3)

    wet_mask = (jnp.arange(BLK)[None, :] < wet_rows[:, None]).astype(jnp.float32).reshape(device_total, 1, RB, BLK)
    slot_mask = (jnp.arange(K)[None, :] < block_count[:, None]).astype(jnp.bfloat16).reshape(device_total, RB, K)
    columns = col_index.reshape(device_total, RB, K).astype(jnp.int32)
    exp_first, exp_second, imp_first, imp_second = [stored.reshape(device_total, RB, K, BLK, BLK) for stored in (exp_month_a, exp_month_b, imp_month_a, imp_month_b)]
    tracer_state = by_device(tracer) * wet_mask
    forcing = by_device(source)
    for step_index in range(STEPS):
        month_now = month_day[step_index]
        rounded = tracer_state.astype(jnp.bfloat16)
        product = apply_blocks(extend_blocks(rounded, send_list), columns, slot_mask, exp_first, exp_second, month_now)
        moved = ((product + forcing) * wet_mask).astype(jnp.bfloat16)
        tracer_state = apply_blocks(extend_blocks(moved, send_list), columns, slot_mask, imp_first, imp_second, month_now) * wet_mask
    return tracer_state.transpose(1, 0, 2, 3).reshape(TRACERS, device_total * RB * BLK)
```

```python
import functools

import jax
import jax.numpy as jnp
from jax import lax
from jax.experimental import pallas as pl
from jax.experimental.pallas import tpu as pltpu
from jax.sharding import PartitionSpec as P

STEPS = 2
DAYS = 30
STRIDE = 4
DIRECTIONS = 4


def swap_pairs(count, groups, stride, parity):
    partner = {}
    for i in range(count - stride):
        if (i // stride) % 2 == parity:
            partner[i], partner[i + stride] = i + stride, i
    idle = [i for i in range(count) if i not in partner]
    for i in idle:
        if i ^ 1 in idle:
            partner[i] = i ^ 1
    pairs = []
    for g in range(groups):
        for i in range(count):
            if i in partner:
                pairs.append((g * count + i, g * count + partner[i]))
            else:
                other = g ^ 1 if g ^ 1 < groups else g
                pairs.append((g * count + i, other * count + i))
    return pairs


def my_flips():
    place = lax.axis_index("rows")
    return 1 - place % 2, 1 - (place // STRIDE) % 2


def direction_of(swap, flips):
    if swap < 2:
        return swap ^ 1 ^ flips[0]
    return 2 + ((swap - 2) ^ 1 ^ flips[1])


def first_kernel(tracer_ref, send_ref, wet_ref, c_ref, o_ref, z_ref, y_ref, buf, sems):
    flips = my_flips()
    block = buf.shape[2]
    rows = [send_ref[0, direction_of(n, flips), 0] for n in range(DIRECTIONS)]
    copies = []
    for n in range(DIRECTIONS):
        start = pl.multiple_of(rows[n] * block, block)
        copy = pltpu.make_async_copy(tracer_ref.at[:, pl.ds(start, block)], buf.at[n], sems.at[n])
        copy.start()
        copies.append(copy)
    lane = lax.broadcasted_iota(jnp.int32, buf.shape[1:], 1)
    for n, out in enumerate((c_ref, o_ref, z_ref, y_ref)):
        copies[n].wait()
        out[...] = jnp.where(lane < wet_ref[rows[n]], buf[n], 0.0).astype(out.dtype)


def blend_kernel(step, a_ref, b_ref, day_ref, out_ref):
    day = day_ref[step]
    late = day.astype(jnp.float32) / DAYS
    early = (DAYS - day).astype(jnp.float32) / DAYS
    row_blocks, slots, block, _ = a_ref.shape

    def one(r, carry):
        for k in range(slots):
            mixed = early * a_ref[r, k].astype(jnp.float32) + late * b_ref[r, k].astype(jnp.float32)
            out_ref[r, :, pl.ds(k * block, block)] = mixed.astype(out_ref.dtype)
        return carry

    lax.fori_loop(0, row_blocks, one, 0)


def apply_kernel(first, explicit, last, *refs):
    refs = list(refs)
    col_ref, count_ref, send_ref, wet_ref, field_ref, matrix_ref = refs[:6]
    halos = refs[6:10]
    refs = refs[10:]
    source_ref = refs.pop(0) if explicit else None
    out_ref = refs.pop(0)
    outgoing = [] if last else refs[:4]
    ext, picked = refs[-2:]
    flips = my_flips()
    row_blocks, slots = col_ref.shape
    block = matrix_ref.shape[1]
    lane = lax.broadcasted_iota(jnp.int32, ext.shape[1:], 1)
    for r in range(row_blocks):
        if first:
            own = field_ref[:, pl.ds(r * block, block)]
            ext[r] = jnp.where(lane < wet_ref[r], own, 0.0).astype(ext.dtype)
        else:
            ext[r] = field_ref[r]
    for n in range(DIRECTIONS):
        ext[row_blocks + n] = halos[n][...]
    nothing = row_blocks + DIRECTIONS
    ext[nothing] = jnp.zeros(ext.shape[1:], ext.dtype)
    for r in range(row_blocks):
        for k in range(slots):
            slot = col_ref[r, k]
            j = slot - row_blocks
            moved = row_blocks + (j ^ jnp.where(j < 2, flips[0], flips[1]))
            place = jnp.where(slot < row_blocks, slot, moved)
            place = jnp.where(k < count_ref[r], place, nothing)
            picked[r, :, pl.ds(k * block, block)] = ext[place]
    for r in range(row_blocks):
        total = lax.dot_general(
            picked[r], matrix_ref[r], (((1,), (1,)), ((), ())), preferred_element_type=jnp.float32
        )
        if explicit:
            total = total + source_ref[:, pl.ds(r * block, block)]
        total = jnp.where(lane < wet_ref[r], total, 0.0)
        if last:
            out_ref[:, pl.ds(r * block, block)] = total
        else:
            out_ref[r] = total.astype(out_ref.dtype)
    for n, out in enumerate(outgoing):
        out[...] = out_ref[send_ref[0, direction_of(n, flips), 0]]


def on_device(swaps, tracer, source, exp_a, exp_b, imp_a, imp_b, col_index, block_count, send_list, wet_rows, month_day):
    tracers, points = tracer.shape
    row_blocks, slots = col_index.shape
    block = points // row_blocks
    half = jnp.bfloat16
    smem = pl.BlockSpec(memory_space=pltpu.SMEM)
    vmem = pl.BlockSpec(memory_space=pltpu.VMEM)
    piece = jax.ShapeDtypeStruct((tracers, block), half)
    params = pltpu.CompilerParams(vmem_limit_bytes=40 * 1024 * 1024)

    outgoing = pl.pallas_call(
        first_kernel,
        out_shape=[piece] * DIRECTIONS,
        in_specs=[pl.BlockSpec(memory_space=pl.ANY), smem, smem],
        out_specs=[vmem] * DIRECTIONS,
        scratch_shapes=[
            pltpu.VMEM((DIRECTIONS, tracers, block), jnp.float32),
            pltpu.SemaphoreType.DMA((DIRECTIONS,)),
        ],
        compiler_params=params,
        name="first_outgoing",
    )(tracer, send_list, wet_rows)

    def blend(a, b, step):
        return pl.pallas_call(
            functools.partial(blend_kernel, step),
            out_shape=jax.ShapeDtypeStruct((row_blocks, block, slots * block), half),
            in_specs=[vmem, vmem, smem],
            out_specs=vmem,
            compiler_params=params,
            name="blend",
        )(a, b, month_day)

    def apply(field, halos, matrix, first, explicit, last):
        operands = [col_index, block_count, send_list, wet_rows, field, matrix, *halos]
        specs = [smem] * 4 + [vmem] * (2 + DIRECTIONS)
        if explicit:
            operands.append(source)
            specs.append(vmem)
        if last:
            shapes = [jax.ShapeDtypeStruct((tracers, points), jnp.float32)]
        else:
            shapes = [jax.ShapeDtypeStruct((row_blocks, tracers, block), half)] + [piece] * DIRECTIONS
        return pl.pallas_call(
            functools.partial(apply_kernel, first, explicit, last),
            out_shape=shapes,
            in_specs=specs,
            out_specs=[vmem] * len(shapes),
            scratch_shapes=[
                pltpu.VMEM((row_blocks + DIRECTIONS + 1, tracers, block), half),
                pltpu.VMEM((row_blocks, tracers, slots * block), half),
            ],
            compiler_params=params,
            name="apply",
        )(*operands)

    def exchange(pieces):
        return [lax.ppermute(p, ("groups", "rows"), s) for p, s in zip(pieces, swaps)]

    field = tracer
    for step in range(STEPS):
        for explicit in (True, False):
            matrix = blend(exp_a, exp_b, step) if explicit else blend(imp_a, imp_b, step)
            last = step == STEPS - 1 and not explicit
            halos = exchange(outgoing)
            field, *outgoing = apply(field, halos, matrix, step == 0 and explicit, explicit, last)
    return field


def solution(mesh):
    count, groups = mesh.shape["rows"], mesh.shape["groups"]
    swaps = [swap_pairs(count, groups, stride, parity) for stride in (1, STRIDE) for parity in (0, 1)]
    wide = P("groups", "rows")
    rows = P("rows")
    return jax.shard_map(
        functools.partial(on_device, swaps),
        mesh=mesh,
        in_specs=(wide, wide, rows, rows, rows, rows, rows, rows, rows, rows, P()),
        out_specs=wide,
        check_vma=False,
    )
```

```python
import functools

import jax
import jax.numpy as jnp
from jax import lax
from jax.experimental import pallas as pl
from jax.experimental.pallas import tpu as pltpu
from jax.sharding import PartitionSpec as P

STEPS = 2
DAYS = 30
STRIDE = 4
DIRECTIONS = 4


def swap_pairs(count, groups, stride, parity):
    partner = {}
    for i in range(count - stride):
        if (i // stride) % 2 == parity:
            partner[i], partner[i + stride] = i + stride, i
    idle = [i for i in range(count) if i not in partner]
    for i in idle:
        if i ^ 1 in idle:
            partner[i] = i ^ 1
    pairs = []
    for g in range(groups):
        for i in range(count):
            if i in partner:
                pairs.append((g * count + i, g * count + partner[i]))
            else:
                other = g ^ 1 if g ^ 1 < groups else g
                pairs.append((g * count + i, other * count + i))
    return pairs


def my_flips():
    place = lax.axis_index("rows")
    return 1 - place % 2, 1 - (place // STRIDE) % 2


def direction_of(swap, flips):
    if swap < 2:
        return swap ^ 1 ^ flips[0]
    return 2 + ((swap - 2) ^ 1 ^ flips[1])


def place_of(slot, row_blocks, flips):
    j = slot - row_blocks
    return jnp.where(slot < row_blocks, slot, row_blocks + (j ^ jnp.where(j < 2, flips[0], flips[1])))


def start_all(copies):
    for copy in copies:
        copy.start()
    return copies


def prologue_kernel(tracer, wet, send, c_out, o_out, z_out, y_out, field, wet_mask, send_pick, raw, wet_s, send_s, sems):
    copies = start_all(
        [
            pltpu.make_async_copy(tracer, raw, sems.at[0]),
            pltpu.make_async_copy(wet, wet_s, sems.at[1]),
            pltpu.make_async_copy(send, send_s, sems.at[2]),
        ]
    )
    flips = my_flips()
    row_blocks = wet.shape[0]
    tracers, points = raw.shape
    block = points // row_blocks
    for copy in copies[::-1]:
        copy.wait()
    rows = [send_s[direction_of(n, flips)] for n in range(DIRECTIONS)]
    lane = lax.broadcasted_iota(jnp.int32, (tracers, block), 1)
    lane8 = lax.broadcasted_iota(jnp.int32, (wet_mask.shape[0], block), 1)
    for r in range(row_blocks):
        columns = pl.ds(r * block, block)
        field[:, columns] = jnp.where(lane < wet_s[r], raw[:, columns], 0.0).astype(field.dtype)
    for n, out in enumerate((c_out, o_out, z_out, y_out)):
        out[...] = field[:, pl.ds(pl.multiple_of(rows[n] * block, block), block)]
    for r in range(row_blocks):
        wet_mask[:, pl.ds(r * block, block)] = jnp.where(lane8 < wet_s[r], 1.0, 0.0)
    for n in range(DIRECTIONS):
        send_pick[n] = jnp.full(send_pick.shape[1:], rows[n], jnp.int32).astype(send_pick.dtype)


def blended(a, b, early, late):
    mixed = early * a.astype(jnp.float32) + late * b.astype(jnp.float32)
    return mixed.astype(a.dtype).T


def add_repeats(table, dense, pairs, block):
    def one(e, carry):
        row = table[pairs + 1 + e]
        columns = pl.ds(pl.multiple_of(row * block, block), block)
        source = pl.ds(pl.multiple_of(table[2 * pairs + 1 + e] * block, block), block)
        target = pl.ds(pl.multiple_of(table[3 * pairs + 1 + e] * block, block), block)
        dense[target, columns] = dense[target, columns] + dense[source, columns]
        return carry

    lax.fori_loop(0, table[pairs], one, 0)


def local_part(field, dense, source, partial):
    total = jnp.dot(field[...], dense[pl.ds(0, field.shape[1]), :], preferred_element_type=jnp.float32)
    partial[...] = total if source is None else total + source[...]


def ready_first_kernel(
    col, count, day, field, source, a, b,
    dense, partial, table_out, weights,
    a_v, b_v, source_v, col_s, count_s, day_s, table, sems,
):
    row_blocks, slots, block, _ = a.shape
    pairs = row_blocks * slots
    index_copies = start_all(
        [
            pltpu.make_async_copy(col, col_s, sems.at[0]),
            pltpu.make_async_copy(count, count_s, sems.at[1]),
            pltpu.make_async_copy(day, day_s, sems.at[2]),
        ]
    )
    month_copies = []
    for r in range(row_blocks):
        month_copies.append(
            start_all(
                [
                    pltpu.make_async_copy(a.at[r], a_v.at[r], sems.at[5 + r]),
                    pltpu.make_async_copy(b.at[r], b_v.at[r], sems.at[5 + row_blocks + r]),
                ]
            )
        )
    source_copy = start_all([pltpu.make_async_copy(source, source_v, sems.at[3])])[0]
    flips = my_flips()
    dense[...] = jnp.zeros(dense.shape, dense.dtype)
    for copy in index_copies:
        copy.wait()
    for step in range(STEPS):
        now = day_s[step]
        for n, days in enumerate((DAYS - now, now)):
            weights[2 * step + n] = jnp.full(weights.shape[1:], days.astype(jnp.float32) * (1.0 / DAYS), jnp.float32)
    unused = row_blocks + DIRECTIONS
    repeats = jnp.int32(0)
    places = {}
    for r in range(row_blocks):
        for k in range(slots):
            slot = col_s[r, k]
            used = k < count_s[r]
            again = jnp.bool_(False)
            for earlier in range(k):
                again = again | (col_s[r, earlier] == slot)
            again = again & used
            target = place_of(slot, row_blocks, flips)
            aside = unused + 1 + k
            place = jnp.where(used, jnp.where(again, aside, target), unused)
            places[r, k] = place
            table[r * slots + k] = place
            table[pairs + 1 + repeats] = jnp.int32(r)
            table[2 * pairs + 1 + repeats] = jnp.int32(aside)
            table[3 * pairs + 1 + repeats] = target
            repeats = repeats + again.astype(jnp.int32)
    table[pairs] = repeats
    table_copy = start_all([pltpu.make_async_copy(table, table_out, sems.at[4])])[0]
    early, late = weights[0, :1], weights[1, :1]
    for r in range(row_blocks):
        for copy in month_copies[r]:
            copy.wait()
        for k in range(slots):
            rows = pl.ds(pl.multiple_of(places[r, k] * block, block), block)
            dense[rows, pl.ds(r * block, block)] = blended(a_v[r, k], b_v[r, k], early, late)
    add_repeats(table, dense, pairs, block)
    source_copy.wait()
    local_part(field, dense, source_v, partial)
    table_copy.wait()


def ready_kernel(step, explicit, *refs):
    refs = list(refs)
    table_in, weights, field, a, b, _ = refs[:6]
    refs = refs[6:]
    source = refs.pop(0) if explicit else None
    dense, partial, stage, table, sem = refs
    row_blocks, slots, block, _ = a.shape
    pairs = row_blocks * slots
    table_copy = pltpu.make_async_copy(table_in, table, sem)
    table_copy.start()
    early, late = weights[2 * step, :1], weights[2 * step + 1, :1]
    staged = stage.shape[0]

    def rows_of(r, k):
        return pl.ds(pl.multiple_of(table[r * slots + k] * block, block), block)

    for r in range(staged):
        for k in range(slots):
            stage[r, k] = blended(a[r, k], b[r, k], early, late)
    table_copy.wait()
    for r in range(row_blocks):
        for k in range(slots):
            value = stage[r, k] if r < staged else blended(a[r, k], b[r, k], early, late)
            dense[rows_of(r, k), pl.ds(r * block, block)] = value
    add_repeats(table, dense, pairs, block)
    local_part(field, dense, source, partial)


def finish_kernel(last, partial, dense, wet_mask, send_pick, c_in, o_in, z_in, y_in, out, *refs):
    tracers, points = partial.shape
    block = c_in.shape[1]
    row_blocks = points // block
    halo = jnp.concatenate([h[...] for h in (c_in, o_in, z_in, y_in)], 1)
    total = partial[...] + jnp.dot(
        halo, dense[pl.ds(points, DIRECTIONS * block), :], preferred_element_type=jnp.float32
    )
    tall = wet_mask.shape[0]
    total = total.reshape(tracers // tall, tall, points) * wet_mask[...][None]
    total = total.reshape(tracers, points)
    if last:
        stage, sem = refs
        stage[...] = total
        copy = pltpu.make_async_copy(stage, out, sem)
        copy.start()
        copy.wait()
        return
    total = total.astype(out.dtype)
    out[...] = total
    tall = send_pick.shape[1]
    blocks = [
        total[:, r * block : (r + 1) * block].reshape(tracers // tall, tall, block) for r in range(row_blocks)
    ]
    for n, outgoing in enumerate(refs):
        wanted = send_pick[n]
        chosen = blocks[0]
        for r in range(1, row_blocks):
            chosen = jnp.where((wanted == r)[None], blocks[r], chosen)
        outgoing[...] = chosen.reshape(tracers, block)


def on_device(swaps, tracer, source, exp_a, exp_b, imp_a, imp_b, col_index, block_count, send_list, wet_rows, month_day):
    tracers, points = tracer.shape
    row_blocks, slots = col_index.shape
    block = points // row_blocks
    pairs = row_blocks * slots
    half, full = jnp.bfloat16, jnp.float32
    hbm = pl.BlockSpec(memory_space=pltpu.HBM)
    vmem = pl.BlockSpec(memory_space=pltpu.VMEM)
    params = pltpu.CompilerParams(vmem_limit_bytes=32 * 1024 * 1024)
    shape = jax.ShapeDtypeStruct
    piece = shape((tracers, block), half)
    field_shape = shape((tracers, points), half)
    partial_shape = shape((tracers, points), full)
    dense_shape = shape(((row_blocks + DIRECTIONS + 1 + slots) * block, points), half)
    table_size = 4 * pairs + 1
    dma = pltpu.SemaphoreType.DMA

    def stay(*arrays):
        return [pltpu.with_memory_space_constraint(x, pltpu.HBM) for x in arrays]

    *outgoing, field, wet_mask, send_pick = pl.pallas_call(
        prologue_kernel,
        out_shape=[piece] * DIRECTIONS
        + [field_shape, shape((8, points), full), shape((DIRECTIONS, 16, block), half)],
        in_specs=[hbm] * 3,
        out_specs=[vmem] * (DIRECTIONS + 3),
        scratch_shapes=[
            pltpu.VMEM((tracers, points), full),
            pltpu.SMEM((row_blocks,), jnp.int32),
            pltpu.SMEM((DIRECTIONS,), jnp.int32),
            dma((3,)),
        ],
        compiler_params=params,
        name="prologue",
    )(*stay(tracer, wet_rows, send_list.reshape(DIRECTIONS)))

    def ready_first(field):
        return pl.pallas_call(
            ready_first_kernel,
            out_shape=[dense_shape, partial_shape, shape((table_size,), jnp.int32), shape((2 * STEPS, 8, block), full)],
            in_specs=[hbm] * 3 + [vmem] + [hbm] * 3,
            out_specs=[vmem] * 4,
            scratch_shapes=[
                pltpu.VMEM(exp_a.shape, half),
                pltpu.VMEM(exp_b.shape, half),
                pltpu.VMEM((tracers, points), full),
                pltpu.SMEM((row_blocks, slots), jnp.int32),
                pltpu.SMEM((row_blocks,), jnp.int32),
                pltpu.SMEM((STEPS,), jnp.int32),
                pltpu.SMEM((table_size,), jnp.int32),
                dma((5 + 2 * row_blocks,)),
            ],
            compiler_params=params,
            name="ready_first",
        )(*stay(col_index, block_count, month_day), field, *stay(source, exp_a, exp_b))

    def ready(step, explicit, table, weights, field, dense):
        a, b = (exp_a, exp_b) if explicit else (imp_a, imp_b)
        operands = [table, weights, field, a, b, dense] + ([source] if explicit else [])
        return pl.pallas_call(
            functools.partial(ready_kernel, step, explicit),
            out_shape=[dense_shape, partial_shape],
            in_specs=[vmem] * len(operands),
            out_specs=[vmem] * 2,
            input_output_aliases={5: 0},
            scratch_shapes=[
                pltpu.VMEM((row_blocks // 2, slots, block, block), half),
                pltpu.SMEM((table_size,), jnp.int32),
                dma(()),
            ],
            compiler_params=params,
            name="ready",
        )(*operands)

    def finish(last, partial, dense, halos):
        return pl.pallas_call(
            functools.partial(finish_kernel, last),
            out_shape=[partial_shape] if last else [field_shape] + [piece] * DIRECTIONS,
            in_specs=[vmem] * (4 + DIRECTIONS),
            out_specs=[hbm] if last else [vmem] * (1 + DIRECTIONS),
            scratch_shapes=[pltpu.VMEM((tracers, points), full), dma(())] if last else [],
            compiler_params=params,
            name="finish",
        )(partial, dense, wet_mask, send_pick, *halos)

    for step in range(STEPS):
        for explicit in (True, False):
            halos = [lax.ppermute(p, ("groups", "rows"), s) for p, s in zip(outgoing, swaps)]
            if step == 0 and explicit:
                dense, partial, table, weights = ready_first(field)
            else:
                dense, partial = ready(step, explicit, table, weights, field, dense)
            last = step == STEPS - 1 and not explicit
            field, *outgoing = finish(last, partial, dense, halos)
    return field


def solution(mesh):
    count, groups = mesh.shape["rows"], mesh.shape["groups"]
    swaps = [swap_pairs(count, groups, stride, parity) for stride in (1, STRIDE) for parity in (0, 1)]
    wide = P("groups", "rows")
    rows = P("rows")
    return jax.shard_map(
        functools.partial(on_device, swaps),
        mesh=mesh,
        in_specs=(wide, wide, rows, rows, rows, rows, rows, rows, rows, rows, P()),
        out_specs=wide,
        check_vma=False,
    )
```

```python
import functools

import jax
import jax.numpy as jnp
from jax import lax
from jax.experimental import pallas as pl
from jax.experimental.pallas import tpu as pltpu
from jax.sharding import PartitionSpec as P

STEPS = 2
DAYS = 30
STRIDE = 4
DIRECTIONS = 4


def swap_pairs(count, groups, stride, parity):
    partner = {}
    for i in range(count - stride):
        if (i // stride) % 2 == parity:
            partner[i], partner[i + stride] = i + stride, i
    idle = [i for i in range(count) if i not in partner]
    for i in idle:
        if i ^ 1 in idle:
            partner[i] = i ^ 1
    pairs = []
    for g in range(groups):
        for i in range(count):
            if i in partner:
                pairs.append((g * count + i, g * count + partner[i]))
            else:
                other = g ^ 1 if g ^ 1 < groups else g
                pairs.append((g * count + i, other * count + i))
    return pairs


def my_flips():
    place = lax.axis_index("rows")
    return 1 - place % 2, 1 - (place // STRIDE) % 2


def direction_of(swap, flips):
    if swap < 2:
        return swap ^ 1 ^ flips[0]
    return 2 + ((swap - 2) ^ 1 ^ flips[1])


def place_of(slot, row_blocks, flips):
    j = slot - row_blocks
    return jnp.where(slot < row_blocks, slot, row_blocks + (j ^ jnp.where(j < 2, flips[0], flips[1])))


def prologue_kernel(
    tracer, wet_in, send_in, col_in, count_in, day_in, source,
    c_out, o_out, z_out, y_out, field, dense, forcing, wet, send, col, count, day,
    raw, sems,
):
    tracers, points = raw.shape
    row_blocks = wet.shape[0]
    block = points // row_blocks
    pairs = ((tracer, raw), (wet_in, wet), (send_in, send), (col_in, col), (count_in, count), (day_in, day), (source, forcing))
    copies = [pltpu.make_async_copy(a, b, sems.at[n]) for n, (a, b) in enumerate(pairs)]
    for copy in copies:
        copy.start()
    used = (row_blocks + DIRECTIONS) * block
    dense[pl.ds(0, used), :] = jnp.zeros((used, points), dense.dtype)
    flips = my_flips()
    for copy in copies[:-1]:
        copy.wait()
    lane = lax.broadcasted_iota(jnp.int32, (tracers, block), 1)
    for n, out in enumerate((c_out, o_out, z_out, y_out)):
        row = send[direction_of(n, flips)]
        piece = raw[:, pl.ds(pl.multiple_of(row * block, block), block)]
        out[...] = jnp.where(lane < wet[row], piece, 0.0).astype(out.dtype)
    for r in range(row_blocks):
        columns = pl.ds(r * block, block)
        field[:, columns] = jnp.where(lane < wet[r], raw[:, columns], 0.0).astype(field.dtype)
    copies[-1].wait()


def blended(a, b, early, late):
    mixed = early * a.astype(jnp.float32) + late * b.astype(jnp.float32)
    return mixed.astype(a.dtype).T


def make_table(col, count, _a, _b, table):
    row_blocks, slots = col.shape
    pairs = row_blocks * slots
    flips = my_flips()
    unused = row_blocks + DIRECTIONS
    repeats = jnp.int32(0)
    for r in range(row_blocks):
        for k in range(slots):
            slot = col[r, k]
            used = k < count[r]
            again = jnp.bool_(False)
            for earlier in range(k):
                again = again | (col[r, earlier] == slot)
            again = again & used
            target = place_of(slot, row_blocks, flips)
            aside = unused + 1 + k
            table[r * slots + k] = jnp.where(used, jnp.where(again, aside, target), unused)
            table[pairs + 1 + repeats] = jnp.int32(r)
            table[2 * pairs + 1 + repeats] = jnp.int32(aside)
            table[3 * pairs + 1 + repeats] = target
            repeats = repeats + again.astype(jnp.int32)
    table[pairs] = repeats


def add_repeats(table, dense, pairs, block):
    def one(e, carry):
        row = table[pairs + 1 + e]
        columns = pl.ds(pl.multiple_of(row * block, block), block)
        source = pl.ds(pl.multiple_of(table[2 * pairs + 1 + e] * block, block), block)
        target = pl.ds(pl.multiple_of(table[3 * pairs + 1 + e] * block, block), block)
        dense[target, columns] = dense[target, columns] + dense[source, columns]
        return carry

    lax.fori_loop(0, table[pairs], one, 0)


def ready_kernel(step, explicit, *refs):
    refs = list(refs)
    day, table, field, a, b, _ = refs[:6]
    refs = refs[6:]
    source = refs.pop(0) if explicit else None
    dense, partial = refs
    row_blocks, slots, block, _ = a.shape
    now = day[step]
    early = (DAYS - now).astype(jnp.float32) * (1.0 / DAYS)
    late = now.astype(jnp.float32) * (1.0 / DAYS)
    for r in range(row_blocks):
        for k in range(slots):
            rows = pl.ds(pl.multiple_of(table[r * slots + k] * block, block), block)
            dense[rows, pl.ds(r * block, block)] = blended(a[r, k], b[r, k], early, late)
    add_repeats(table, dense, row_blocks * slots, block)
    total = jnp.dot(field[...], dense[pl.ds(0, field.shape[1]), :], preferred_element_type=jnp.float32)
    partial[...] = total + source[...] if explicit else total


def finish_kernel(last, wet, send, partial, dense, c_in, o_in, z_in, y_in, out, *refs):
    tracers, points = partial.shape
    block = c_in.shape[1]
    row_blocks = points // block
    halo = jnp.concatenate([h[...] for h in (c_in, o_in, z_in, y_in)], 1)
    total = partial[...] + jnp.dot(
        halo, dense[pl.ds(points, DIRECTIONS * block), :], preferred_element_type=jnp.float32
    )
    lane = lax.broadcasted_iota(jnp.int32, (tracers, block), 1)
    target = refs[0] if last else out
    for r in range(row_blocks):
        columns = slice(r * block, (r + 1) * block)
        target[:, columns] = jnp.where(lane < wet[r], total[:, columns], 0.0).astype(target.dtype)
    if last:
        copy = pltpu.make_async_copy(target, out, refs[1])
        copy.start()
        copy.wait()
        return
    flips = my_flips()
    for n, outgoing in enumerate(refs):
        row = send[direction_of(n, flips)]
        outgoing[...] = out[:, pl.ds(pl.multiple_of(row * block, block), block)]


def on_device(swaps, tracer, source, exp_a, exp_b, imp_a, imp_b, col_index, block_count, send_list, wet_rows, month_day):
    tracers, points = tracer.shape
    row_blocks, slots = col_index.shape
    block = points // row_blocks
    half, full, whole = jnp.bfloat16, jnp.float32, jnp.int32
    hbm = pl.BlockSpec(memory_space=pltpu.HBM)
    vmem = pl.BlockSpec(memory_space=pltpu.VMEM)
    smem = pl.BlockSpec(memory_space=pltpu.SMEM)
    params = pltpu.CompilerParams(vmem_limit_bytes=32 * 1024 * 1024)
    shape = jax.ShapeDtypeStruct
    piece = shape((tracers, block), half)
    field_shape = shape((tracers, points), half)
    partial_shape = shape((tracers, points), full)
    dense_shape = shape(((row_blocks + DIRECTIONS + 1 + slots) * block, points), half)
    dma = pltpu.SemaphoreType.DMA

    def stay(*arrays):
        return [pltpu.with_memory_space_constraint(x, pltpu.HBM) for x in arrays]

    indices = [wet_rows, send_list.reshape(DIRECTIONS), col_index, block_count, month_day]
    *outgoing, field, dense, forcing, wet, send, col, count, day = pl.pallas_call(
        prologue_kernel,
        out_shape=[piece] * DIRECTIONS
        + [field_shape, dense_shape, partial_shape]
        + [pltpu.SMEM(x.shape, whole) for x in indices],
        in_specs=[hbm] * 7,
        out_specs=[vmem] * (DIRECTIONS + 3) + [smem] * 5,
        scratch_shapes=[pltpu.VMEM((tracers, points), full), dma((7,))],
        compiler_params=params,
        name="prologue",
    )(*stay(tracer, *indices, source))

    table = pl.pallas_call(
        make_table,
        out_shape=pltpu.SMEM((4 * row_blocks * slots + 1,), whole),
        in_specs=[smem] * 2 + [hbm] * 2,
        out_specs=smem,
        compiler_params=params,
        name="make_table",
    )(col, count, *stay(exp_a, exp_b))

    def ready(step, explicit, field, dense):
        a, b = (exp_a, exp_b) if explicit else (imp_a, imp_b)
        operands = [day, table, field, a, b, dense] + ([forcing] if explicit else [])
        return pl.pallas_call(
            functools.partial(ready_kernel, step, explicit),
            out_shape=[dense_shape, partial_shape],
            in_specs=[smem] * 2 + [vmem] * (len(operands) - 2),
            out_specs=[vmem] * 2,
            input_output_aliases={5: 0},
            compiler_params=params,
            name="ready",
        )(*operands)

    def finish(last, partial, dense, halos):
        return pl.pallas_call(
            functools.partial(finish_kernel, last),
            out_shape=[partial_shape] if last else [field_shape] + [piece] * DIRECTIONS,
            in_specs=[smem] * 2 + [vmem] * (2 + DIRECTIONS),
            out_specs=[hbm] if last else [vmem] * (1 + DIRECTIONS),
            scratch_shapes=[pltpu.VMEM((tracers, points), full), dma(())] if last else [],
            compiler_params=params,
            name="finish",
        )(wet, send, partial, dense, *halos)

    for step in range(STEPS):
        for explicit in (True, False):
            halos = [lax.ppermute(p, ("groups", "rows"), s) for p, s in zip(outgoing, swaps)]
            dense, partial = ready(step, explicit, field, dense)
            last = step == STEPS - 1 and not explicit
            field, *outgoing = finish(last, partial, dense, halos)
    return field


def solution(mesh):
    count, groups = mesh.shape["rows"], mesh.shape["groups"]
    swaps = [swap_pairs(count, groups, stride, parity) for stride in (1, STRIDE) for parity in (0, 1)]
    wide = P("groups", "rows")
    rows = P("rows")
    return jax.shard_map(
        functools.partial(on_device, swaps),
        mesh=mesh,
        in_specs=(wide, wide, rows, rows, rows, rows, rows, rows, rows, rows, P()),
        out_specs=wide,
        check_vma=False,
    )
```

```python
import functools

import jax
import jax.numpy as jnp
from jax import lax
from jax.experimental import pallas as pl
from jax.experimental.pallas import tpu as pltpu
from jax.sharding import PartitionSpec as P

STEPS = 2
DAYS = 30
STRIDE = 4
DIRECTIONS = 4
GROUP = 3
PARTS = 2
AHEAD = (0, 4, 4, 4, 0)
SWAPS = ((1, 1), (STRIDE, 0), (STRIDE, 1), (1, 0))


def swap_pairs(count, groups, stride, parity):
    partner = {}
    for i in range(count - stride):
        if (i // stride) % 2 == parity:
            partner[i], partner[i + stride] = i + stride, i
    idle = [i for i in range(count) if i not in partner]
    for i in idle:
        if i ^ 1 in idle:
            partner[i] = i ^ 1
    pairs = []
    for g in range(groups):
        for i in range(count):
            if i in partner:
                pairs.append((g * count + i, g * count + partner[i]))
            else:
                other = g ^ 1 if g ^ 1 < groups else g
                pairs.append((g * count + i, other * count + i))
    return pairs


def direction_of(swap):
    stride, parity = SWAPS[swap]
    up = (lax.axis_index("rows") // stride) % 2 == parity
    return jnp.where(up, 0, 1) + (0 if stride == 1 else 2)


def halo_places(row_blocks):
    places = []
    for direction in range(DIRECTIONS):
        stride = 1 if direction < 2 else STRIDE
        mine = (lax.axis_index("rows") // stride) % 2
        parity = mine if direction % 2 else 1 - mine
        even, odd = (row_blocks + SWAPS.index((stride, p)) for p in (0, 1))
        places.append(jnp.where(parity == 0, even, odd))
    return places


def place_of(slot, row_blocks, halos):
    place = slot
    for direction in range(DIRECTIONS):
        place = jnp.where(slot == row_blocks + direction, halos[direction], place)
    return place


def prologue_kernel(
    tracer, wet_in, send_in, col_in, count_in, day_in, source,
    out_0, out_1, out_2, out_3, field, dense, later, forcing, wet, send, col, count, day,
    raw, sems,
):
    tracers, points = raw.shape
    row_blocks = wet.shape[0]
    block = points // row_blocks
    pairs = ((tracer, raw), (wet_in, wet), (send_in, send), (col_in, col), (count_in, count), (day_in, day), (source, forcing))
    copies = [pltpu.make_async_copy(a, b, sems.at[n]) for n, (a, b) in enumerate(pairs)]
    for copy in copies:
        copy.start()
    used = (row_blocks + DIRECTIONS) * block
    for empty in (dense, later):
        empty[pl.ds(0, used), :] = jnp.zeros((used, points), empty.dtype)
    for copy in copies[:-1]:
        copy.wait()
    lane = lax.broadcasted_iota(jnp.int32, (tracers, block), 1)
    for n, out in enumerate((out_0, out_1, out_2, out_3)):
        row = send[direction_of(n)]
        piece = raw[:, pl.ds(pl.multiple_of(row * block, block), block)]
        out[...] = jnp.where(lane < wet[row], piece, 0.0).astype(out.dtype)
    for r in range(row_blocks):
        columns = pl.ds(r * block, block)
        field[:, columns] = jnp.where(lane < wet[r], raw[:, columns], 0.0).astype(field.dtype)
    copies[-1].wait()


def blended(a, b, early, late):
    mixed = early * a.astype(jnp.float32) + late * b.astype(jnp.float32)
    return mixed.astype(a.dtype).T


def make_table(col, count, _a, _b, _c, _d, table):
    row_blocks, slots = col.shape
    pairs = row_blocks * slots
    halos = halo_places(row_blocks)
    unused = row_blocks + DIRECTIONS
    seconds, others = jnp.int32(0), jnp.int32(0)

    def append(length, first, entry):
        for n, value in enumerate(entry):
            table[(first + n) * pairs + 2 + length] = value

    for r in range(row_blocks):
        known = []
        for k in range(slots):
            slot = col[r, k]
            used = k < count[r]
            aside = unused + 1 + k
            again, rest, later = jnp.bool_(False), jnp.int32(aside), jnp.bool_(False)
            for slot_before, again_before, rest_before in known:
                same = slot_before == slot
                again = again | same
                later = later | (same & again_before)
                rest = jnp.where(same & again_before, rest_before, rest)
            again, later = again & used, later & used
            known.append((slot, again, rest))
            target = place_of(slot, row_blocks, halos)
            table[r * slots + k] = jnp.where(used, jnp.where(again, aside, target), unused)
            entry = (jnp.int32(r), jnp.int32(aside), target)
            append(seconds, 1, entry)
            append(others, 4, (*entry, rest))
            seconds = seconds + (again & ~later).astype(jnp.int32)
            others = others + later.astype(jnp.int32)
    table[pairs] = seconds
    table[pairs + 1] = others
    for n in range(GROUP - 1):
        append(seconds + n, 1, (jnp.int32(0), jnp.int32(unused), jnp.int32(unused)))


def add_repeats(table, dense, pairs, block):
    size = block // PARTS
    parts = range(0, block, size)

    def entry(first, length, e):
        row, *places = [table[(first + n) * pairs + 2 + e] for n in range(length)]
        columns = pl.ds(pl.multiple_of(row * block, block), block)
        return [[(pl.ds(pl.multiple_of(p * block + part, size), size), columns) for p in places] for part in parts]

    def added(*places):
        total = dense[places[0]].astype(jnp.float32)
        for place in places[1:]:
            total = total + dense[place].astype(jnp.float32)
        rounded = total.astype(dense.dtype)
        return rounded, (total - rounded.astype(jnp.float32)).astype(dense.dtype)

    def group(g, carry):
        for entries in zip(*[entry(1, 3, g * GROUP + n) for n in range(GROUP)]):
            sums = [added(target, aside) for aside, target in entries]
            for (aside, target), (rounded, rest) in zip(entries, sums):
                dense[target] = rounded
                dense[aside] = rest
        return carry

    def one(e, carry):
        for aside, target, kept in entry(4, 4, e):
            rounded, rest = added(target, aside, kept)
            dense[target] = rounded
            dense[kept] = rest
        return carry

    lax.fori_loop(0, (table[pairs] + GROUP - 1) // GROUP, group, 0)
    lax.fori_loop(0, table[pairs + 1], one, 0)


def month_weights(day, step):
    now = day[step]
    return (DAYS - now).astype(jnp.float32) * (1.0 / DAYS), now.astype(jnp.float32) * (1.0 / DAYS)


def lay_out(a, b, weights, table, dense, rows):
    slots, block = a.shape[1:3]
    for r in rows:
        for k in range(slots):
            place = pl.ds(pl.multiple_of(table[r * slots + k] * block, block), block)
            dense[place, pl.ds(r * block, block)] = blended(a[r, k], b[r, k], *weights)


def ready_kernel(apply, *refs):
    refs = list(refs)
    explicit, more = apply % 2 == 0, apply + 1 < 2 * STEPS
    day, table, field, a, b, dense = [refs.pop(0) for _ in range(6)]
    next_a, next_b, _ = [refs.pop(0) for _ in range(3)] if more else (None, None, None)
    forcing = refs.pop(0) if explicit else None
    dense, partial = refs[:2]
    row_blocks, slots, block, _ = a.shape
    done, ahead = [row_blocks * share // 8 for share in (AHEAD[apply], AHEAD[apply + 1])]
    lay_out(a, b, month_weights(day, apply // 2), table, dense, range(done, row_blocks))
    add_repeats(table, dense, row_blocks * slots, block)
    total = jnp.dot(field[...], dense[pl.ds(0, field.shape[1]), :], preferred_element_type=jnp.float32)
    partial[...] = total + forcing[...] if explicit else total
    if more:
        lay_out(next_a, next_b, month_weights(day, (apply + 1) // 2), table, refs[2], range(ahead))


def finish_kernel(last, wet, send, partial, dense, in_0, in_1, in_2, in_3, out, *refs):
    tracers, points = partial.shape
    block = in_0.shape[1]
    row_blocks = points // block
    halo = jnp.concatenate([h[...] for h in (in_0, in_1, in_2, in_3)], 1)
    total = partial[...] + jnp.dot(
        halo, dense[pl.ds(points, DIRECTIONS * block), :], preferred_element_type=jnp.float32
    )
    lane = lax.broadcasted_iota(jnp.int32, (tracers, block), 1)
    target = refs[0] if last else out
    for r in range(row_blocks):
        columns = slice(r * block, (r + 1) * block)
        target[:, columns] = jnp.where(lane < wet[r], total[:, columns], 0.0).astype(target.dtype)
    if last:
        copy = pltpu.make_async_copy(target, out, refs[1])
        copy.start()
        copy.wait()
        return
    for n, outgoing in enumerate(refs):
        row = send[direction_of(n)]
        outgoing[...] = out[:, pl.ds(pl.multiple_of(row * block, block), block)]


def on_device(swaps, tracer, source, exp_a, exp_b, imp_a, imp_b, col_index, block_count, send_list, wet_rows, month_day):
    tracers, points = tracer.shape
    row_blocks, slots = col_index.shape
    block = points // row_blocks
    half, full, whole = jnp.bfloat16, jnp.float32, jnp.int32
    hbm = pl.BlockSpec(memory_space=pltpu.HBM)
    vmem = pl.BlockSpec(memory_space=pltpu.VMEM)
    smem = pl.BlockSpec(memory_space=pltpu.SMEM)
    params = pltpu.CompilerParams(vmem_limit_bytes=32 * 1024 * 1024)
    shape = jax.ShapeDtypeStruct
    piece = shape((tracers, block), half)
    field_shape = shape((tracers, points), half)
    partial_shape = shape((tracers, points), full)
    dense_shape = shape(((row_blocks + DIRECTIONS + 1 + slots) * block, points), half)
    dma = pltpu.SemaphoreType.DMA

    def stay(*arrays):
        return [pltpu.with_memory_space_constraint(x, pltpu.HBM) for x in arrays]

    indices = [wet_rows, send_list.reshape(DIRECTIONS), col_index, block_count, month_day]
    *outgoing, field, dense, later, forcing, wet, send, col, count, day = pl.pallas_call(
        prologue_kernel,
        out_shape=[piece] * DIRECTIONS
        + [field_shape, dense_shape, dense_shape, partial_shape]
        + [pltpu.SMEM(x.shape, whole) for x in indices],
        in_specs=[hbm] * 7,
        out_specs=[vmem] * (DIRECTIONS + 4) + [smem] * 5,
        scratch_shapes=[pltpu.VMEM((tracers, points), full), dma((7,))],
        compiler_params=params,
        name="prologue",
    )(*stay(tracer, *indices, source))

    table = pl.pallas_call(
        make_table,
        out_shape=pltpu.SMEM((8 * row_blocks * slots + 2,), whole),
        in_specs=[smem] * 2 + [hbm] * 4,
        out_specs=smem,
        compiler_params=params,
        name="make_table",
    )(col, count, *stay(exp_a, exp_b, imp_a, imp_b))

    def ready(apply, field, dense, later):
        explicit, more = apply % 2 == 0, apply + 1 < 2 * STEPS
        mine, other = ((exp_a, exp_b), (imp_a, imp_b))[:: 1 if explicit else -1]
        operands = [day, table, field, *mine, dense]
        aliases = {5: 0}
        if more:
            operands += [*other, later]
            aliases[8] = 2
        if explicit:
            operands.append(forcing)
        return pl.pallas_call(
            functools.partial(ready_kernel, apply),
            out_shape=[dense_shape, partial_shape] + [dense_shape] * more,
            in_specs=[smem] * 2 + [vmem] * (len(operands) - 2),
            out_specs=[vmem] * (2 + more),
            input_output_aliases=aliases,
            compiler_params=params,
            name="ready",
        )(*operands)

    def finish(last, partial, dense, halos):
        return pl.pallas_call(
            functools.partial(finish_kernel, last),
            out_shape=[partial_shape] if last else [field_shape] + [piece] * DIRECTIONS,
            in_specs=[smem] * 2 + [vmem] * (2 + DIRECTIONS),
            out_specs=[hbm] if last else [vmem] * (1 + DIRECTIONS),
            scratch_shapes=[pltpu.VMEM((tracers, points), full), dma(())] if last else [],
            compiler_params=params,
            name="finish",
        )(wet, send, partial, dense, *halos)

    for apply in range(2 * STEPS):
        halos = [lax.ppermute(p, ("groups", "rows"), s) for p, s in zip(outgoing, swaps)]
        dense, partial, *begun = ready(apply, field, dense, later)
        field, *outgoing = finish(apply + 1 == 2 * STEPS, partial, dense, halos)
        dense, later = begun[0] if begun else None, dense
    return field


def solution(mesh):
    count, groups = mesh.shape["rows"], mesh.shape["groups"]
    swaps = [swap_pairs(count, groups, stride, parity) for stride, parity in SWAPS]
    wide = P("groups", "rows")
    rows = P("rows")
    return jax.shard_map(
        functools.partial(on_device, swaps),
        mesh=mesh,
        in_specs=(wide, wide, rows, rows, rows, rows, rows, rows, rows, rows, P()),
        out_specs=wide,
        check_vma=False,
    )
```

```python
import functools

import jax
import jax.numpy as jnp
from jax import lax
from jax.experimental import pallas as pl
from jax.experimental.pallas import tpu as pltpu
from jax.sharding import PartitionSpec as P

STEPS = 2
DAYS = 30
STRIDE = 4
DIRECTIONS = 4
GROUP = 3
PARTS = 2
AHEAD = (0, 4, 4, 4, 0)
SWAPS = ((1, 1), (STRIDE, 0), (STRIDE, 1), (1, 0))
ORDERS = ((2, 0, 1, 3), (0, 1, 2, 3), (0, 1, 2, 3), (0, 1, 2, 3))


def swap_pairs(count, groups, stride, parity):
    partner = {}
    for i in range(count - stride):
        if (i // stride) % 2 == parity:
            partner[i], partner[i + stride] = i + stride, i
    idle = [i for i in range(count) if i not in partner]
    for i in idle:
        if i ^ 1 in idle:
            partner[i] = i ^ 1
    pairs = []
    for g in range(groups):
        for i in range(count):
            if i in partner:
                pairs.append((g * count + i, g * count + partner[i]))
            else:
                other = g ^ 1 if g ^ 1 < groups else g
                pairs.append((g * count + i, other * count + i))
    return pairs


def direction_of(swap):
    stride, parity = SWAPS[swap]
    up = (lax.axis_index("rows") // stride) % 2 == parity
    return jnp.where(up, 0, 1) + (0 if stride == 1 else 2)


def halo_places(row_blocks):
    places = []
    for direction in range(DIRECTIONS):
        stride = 1 if direction < 2 else STRIDE
        mine = (lax.axis_index("rows") // stride) % 2
        parity = mine if direction % 2 else 1 - mine
        even, odd = (row_blocks + SWAPS.index((stride, p)) for p in (0, 1))
        places.append(jnp.where(parity == 0, even, odd))
    return places


def place_of(slot, row_blocks, halos):
    place = slot
    for direction in range(DIRECTIONS):
        place = jnp.where(slot == row_blocks + direction, halos[direction], place)
    return place


def prologue_kernel(
    tracer, wet_in, send_in, col_in, count_in, day_in, source,
    out_0, out_1, out_2, out_3, field, dense, later, forcing, wet, send, col, count, day,
    raw, sems,
):
    tracers, points = raw.shape
    row_blocks = wet.shape[0]
    block = points // row_blocks
    pairs = ((tracer, raw), (wet_in, wet), (send_in, send), (col_in, col), (count_in, count), (day_in, day), (source, forcing))
    copies = [pltpu.make_async_copy(a, b, sems.at[n]) for n, (a, b) in enumerate(pairs)]
    for copy in copies:
        copy.start()
    used = (row_blocks + DIRECTIONS) * block
    for empty in (dense, later):
        empty[pl.ds(0, used), :] = jnp.zeros((used, points), empty.dtype)
    for copy in copies[:-1]:
        copy.wait()
    lane = lax.broadcasted_iota(jnp.int32, (tracers, block), 1)
    for n, out in zip(ORDERS[0], (out_0, out_1, out_2, out_3)):
        row = send[direction_of(n)]
        piece = raw[:, pl.ds(pl.multiple_of(row * block, block), block)]
        out[...] = jnp.where(lane < wet[row], piece, 0.0).astype(out.dtype)
    for r in range(row_blocks):
        columns = pl.ds(r * block, block)
        field[:, columns] = jnp.where(lane < wet[r], raw[:, columns], 0.0).astype(field.dtype)
    copies[-1].wait()


def blended(a, b, early, late):
    mixed = early * a.astype(jnp.float32) + late * b.astype(jnp.float32)
    return mixed.astype(a.dtype).T


def make_table(col, count, _a, _b, _c, _d, table):
    row_blocks, slots = col.shape
    pairs = row_blocks * slots
    halos = halo_places(row_blocks)
    unused = row_blocks + DIRECTIONS
    seconds, others = jnp.int32(0), jnp.int32(0)

    def append(length, first, entry):
        for n, value in enumerate(entry):
            table[(first + n) * pairs + 2 + length] = value

    for r in range(row_blocks):
        known = []
        for k in range(slots):
            slot = col[r, k]
            used = k < count[r]
            aside = unused + 1 + k
            again, rest, later = jnp.bool_(False), jnp.int32(aside), jnp.bool_(False)
            for slot_before, again_before, rest_before in known:
                same = slot_before == slot
                again = again | same
                later = later | (same & again_before)
                rest = jnp.where(same & again_before, rest_before, rest)
            again, later = again & used, later & used
            known.append((slot, again, rest))
            target = place_of(slot, row_blocks, halos)
            table[r * slots + k] = jnp.where(used, jnp.where(again, aside, target), unused)
            entry = (jnp.int32(r), jnp.int32(aside), target)
            append(seconds, 1, entry)
            append(others, 4, (*entry, rest))
            seconds = seconds + (again & ~later).astype(jnp.int32)
            others = others + later.astype(jnp.int32)
    table[pairs] = seconds
    table[pairs + 1] = others
    for n in range(GROUP - 1):
        append(seconds + n, 1, (jnp.int32(0), jnp.int32(unused), jnp.int32(unused)))


def add_repeats(table, dense, pairs, block):
    size = block // PARTS
    parts = range(0, block, size)

    def entry(first, length, e):
        row, *places = [table[(first + n) * pairs + 2 + e] for n in range(length)]
        columns = pl.ds(pl.multiple_of(row * block, block), block)
        return [[(pl.ds(pl.multiple_of(p * block + part, size), size), columns) for p in places] for part in parts]

    def added(*places):
        total = dense[places[0]].astype(jnp.float32)
        for place in places[1:]:
            total = total + dense[place].astype(jnp.float32)
        rounded = total.astype(dense.dtype)
        return rounded, (total - rounded.astype(jnp.float32)).astype(dense.dtype)

    def group(g, carry):
        for entries in zip(*[entry(1, 3, g * GROUP + n) for n in range(GROUP)]):
            sums = [added(target, aside) for aside, target in entries]
            for (aside, target), (rounded, rest) in zip(entries, sums):
                dense[target] = rounded
                dense[aside] = rest
        return carry

    def one(e, carry):
        for aside, target, kept in entry(4, 4, e):
            rounded, rest = added(target, aside, kept)
            dense[target] = rounded
            dense[kept] = rest
        return carry

    lax.fori_loop(0, (table[pairs] + GROUP - 1) // GROUP, group, 0)
    lax.fori_loop(0, table[pairs + 1], one, 0)


def month_weights(day, step):
    now = day[step]
    return (DAYS - now).astype(jnp.float32) * (1.0 / DAYS), now.astype(jnp.float32) * (1.0 / DAYS)


def lay_out(a, b, weights, table, dense, rows):
    slots, block = a.shape[1:3]
    for r in rows:
        for k in range(slots):
            place = pl.ds(pl.multiple_of(table[r * slots + k] * block, block), block)
            dense[place, pl.ds(r * block, block)] = blended(a[r, k], b[r, k], *weights)


def ready_kernel(apply, *refs):
    refs = list(refs)
    explicit, more = apply % 2 == 0, apply + 1 < 2 * STEPS
    day, table, field, a, b, dense = [refs.pop(0) for _ in range(6)]
    next_a, next_b, _ = [refs.pop(0) for _ in range(3)] if more else (None, None, None)
    forcing = refs.pop(0) if explicit else None
    dense, partial = refs[:2]
    row_blocks, slots, block, _ = a.shape
    done, ahead = [row_blocks * share // 8 for share in (AHEAD[apply], AHEAD[apply + 1])]
    lay_out(a, b, month_weights(day, apply // 2), table, dense, range(done, row_blocks))
    add_repeats(table, dense, row_blocks * slots, block)
    total = jnp.dot(field[...], dense[pl.ds(0, field.shape[1]), :], preferred_element_type=jnp.float32)
    partial[...] = total + forcing[...] if explicit else total
    if more:
        lay_out(next_a, next_b, month_weights(day, (apply + 1) // 2), table, refs[2], range(ahead))


def finish_kernel(apply, wet, send, partial, dense, in_0, in_1, in_2, in_3, out, *refs):
    tracers, points = partial.shape
    block = in_0.shape[1]
    row_blocks = points // block
    last = apply + 1 == 2 * STEPS
    halos = dict(zip(ORDERS[apply], (in_0, in_1, in_2, in_3)))
    halo = jnp.concatenate([halos[n][...] for n in range(DIRECTIONS)], 1)
    total = partial[...] + jnp.dot(
        halo, dense[pl.ds(points, DIRECTIONS * block), :], preferred_element_type=jnp.float32
    )
    lane = lax.broadcasted_iota(jnp.int32, (tracers, block), 1)
    target = refs[0] if last else out
    for r in range(row_blocks):
        columns = slice(r * block, (r + 1) * block)
        target[:, columns] = jnp.where(lane < wet[r], total[:, columns], 0.0).astype(target.dtype)
    if last:
        copy = pltpu.make_async_copy(target, out, refs[1])
        copy.start()
        copy.wait()
        return
    for n, outgoing in zip(ORDERS[apply + 1], refs):
        row = send[direction_of(n)]
        outgoing[...] = out[:, pl.ds(pl.multiple_of(row * block, block), block)]


def on_device(swaps, tracer, source, exp_a, exp_b, imp_a, imp_b, col_index, block_count, send_list, wet_rows, month_day):
    tracers, points = tracer.shape
    row_blocks, slots = col_index.shape
    block = points // row_blocks
    half, full, whole = jnp.bfloat16, jnp.float32, jnp.int32
    hbm = pl.BlockSpec(memory_space=pltpu.HBM)
    vmem = pl.BlockSpec(memory_space=pltpu.VMEM)
    smem = pl.BlockSpec(memory_space=pltpu.SMEM)
    params = pltpu.CompilerParams(vmem_limit_bytes=32 * 1024 * 1024)
    shape = jax.ShapeDtypeStruct
    piece = shape((tracers, block), half)
    field_shape = shape((tracers, points), half)
    partial_shape = shape((tracers, points), full)
    dense_shape = shape(((row_blocks + DIRECTIONS + 1 + slots) * block, points), half)
    dma = pltpu.SemaphoreType.DMA

    def stay(*arrays):
        return [pltpu.with_memory_space_constraint(x, pltpu.HBM) for x in arrays]

    indices = [wet_rows, send_list.reshape(DIRECTIONS), col_index, block_count, month_day]
    *outgoing, field, dense, later, forcing, wet, send, col, count, day = pl.pallas_call(
        prologue_kernel,
        out_shape=[piece] * DIRECTIONS
        + [field_shape, dense_shape, dense_shape, partial_shape]
        + [pltpu.SMEM(x.shape, whole) for x in indices],
        in_specs=[hbm] * 7,
        out_specs=[vmem] * (DIRECTIONS + 4) + [smem] * 5,
        scratch_shapes=[pltpu.VMEM((tracers, points), full), dma((7,))],
        compiler_params=params,
        name="prologue",
    )(*stay(tracer, *indices, source))

    table = pl.pallas_call(
        make_table,
        out_shape=pltpu.SMEM((8 * row_blocks * slots + 2,), whole),
        in_specs=[smem] * 2 + [hbm] * 4,
        out_specs=smem,
        compiler_params=params,
        name="make_table",
    )(col, count, *stay(exp_a, exp_b, imp_a, imp_b))

    def ready(apply, field, dense, later):
        explicit, more = apply % 2 == 0, apply + 1 < 2 * STEPS
        mine, other = ((exp_a, exp_b), (imp_a, imp_b))[:: 1 if explicit else -1]
        operands = [day, table, field, *mine, dense]
        aliases = {5: 0}
        if more:
            operands += [*other, later]
            aliases[8] = 2
        if explicit:
            operands.append(forcing)
        return pl.pallas_call(
            functools.partial(ready_kernel, apply),
            out_shape=[dense_shape, partial_shape] + [dense_shape] * more,
            in_specs=[smem] * 2 + [vmem] * (len(operands) - 2),
            out_specs=[vmem] * (2 + more),
            input_output_aliases=aliases,
            compiler_params=params,
            name="ready",
        )(*operands)

    def finish(apply, partial, dense, halos):
        last = apply + 1 == 2 * STEPS
        return pl.pallas_call(
            functools.partial(finish_kernel, apply),
            out_shape=[partial_shape] if last else [field_shape] + [piece] * DIRECTIONS,
            in_specs=[smem] * 2 + [vmem] * (2 + DIRECTIONS),
            out_specs=[hbm] if last else [vmem] * (1 + DIRECTIONS),
            scratch_shapes=[pltpu.VMEM((tracers, points), full), dma(())] if last else [],
            compiler_params=params,
            name="finish",
        )(wet, send, partial, dense, *halos)

    for apply in range(2 * STEPS):
        halos = [lax.ppermute(p, ("groups", "rows"), swaps[n]) for p, n in zip(outgoing, ORDERS[apply])]
        dense, partial, *begun = ready(apply, field, dense, later)
        field, *outgoing = finish(apply, partial, dense, halos)
        dense, later = begun[0] if begun else None, dense
    return field


def solution(mesh):
    count, groups = mesh.shape["rows"], mesh.shape["groups"]
    swaps = [swap_pairs(count, groups, stride, parity) for stride, parity in SWAPS]
    wide = P("groups", "rows")
    rows = P("rows")
    return jax.shard_map(
        functools.partial(on_device, swaps),
        mesh=mesh,
        in_specs=(wide, wide, rows, rows, rows, rows, rows, rows, rows, rows, P()),
        out_specs=wide,
        check_vma=False,
    )
```

```python
import functools

import jax
import jax.numpy as jnp
from jax import lax
from jax.experimental import pallas as pl
from jax.experimental.pallas import tpu as pltpu
from jax.sharding import PartitionSpec as P

STEPS = 2
DAYS = 30
STRIDE = 4
DIRECTIONS = 4
GROUP = 2
PARTS = 2
AHEAD = (0, 4, 4, 4, 0)
SWAPS = ((1, 1), (STRIDE, 0), (STRIDE, 1), (1, 0))


def swap_pairs(count, groups, stride, parity):
    partner = {}
    for i in range(count - stride):
        if (i // stride) % 2 == parity:
            partner[i], partner[i + stride] = i + stride, i
    idle = [i for i in range(count) if i not in partner]
    for i in idle:
        if i ^ 1 in idle:
            partner[i] = i ^ 1
    pairs = []
    for g in range(groups):
        for i in range(count):
            if i in partner:
                pairs.append((g * count + i, g * count + partner[i]))
            else:
                other = g ^ 1 if g ^ 1 < groups else g
                pairs.append((g * count + i, other * count + i))
    return pairs


def direction_of(swap):
    stride, parity = SWAPS[swap]
    up = (lax.axis_index("rows") // stride) % 2 == parity
    return jnp.where(up, 0, 1) + (0 if stride == 1 else 2)


def halo_places(row_blocks):
    places = []
    for direction in range(DIRECTIONS):
        stride = 1 if direction < 2 else STRIDE
        mine = (lax.axis_index("rows") // stride) % 2
        parity = mine if direction % 2 else 1 - mine
        even, odd = (row_blocks + SWAPS.index((stride, p)) for p in (0, 1))
        places.append(jnp.where(parity == 0, even, odd))
    return places


def place_of(slot, row_blocks, halos):
    place = slot
    for direction in range(DIRECTIONS):
        place = jnp.where(slot == row_blocks + direction, halos[direction], place)
    return place


def prologue_kernel(
    tracer, wet_in, send_in, col_in, count_in, day_in, source,
    out_0, out_1, out_2, out_3, field, dense, later, forcing, wet, send, col, count, day,
    raw, sems,
):
    tracers, points = raw.shape
    row_blocks = wet.shape[0]
    block = points // row_blocks
    pairs = ((tracer, raw), (wet_in, wet), (send_in, send), (col_in, col), (count_in, count), (day_in, day), (source, forcing))
    copies = [pltpu.make_async_copy(a, b, sems.at[n]) for n, (a, b) in enumerate(pairs)]
    for copy in copies:
        copy.start()
    used = (row_blocks + DIRECTIONS) * block
    for empty in (dense, later):
        empty[pl.ds(0, used), :] = jnp.zeros((used, points), empty.dtype)
    for copy in copies[:-1]:
        copy.wait()
    lane = lax.broadcasted_iota(jnp.int32, (tracers, block), 1)
    for n, out in enumerate((out_0, out_1, out_2, out_3)):
        row = send[direction_of(n)]
        piece = raw[:, pl.ds(pl.multiple_of(row * block, block), block)]
        out[...] = jnp.where(lane < wet[row], piece, 0.0).astype(out.dtype)
    for r in range(row_blocks):
        columns = pl.ds(r * block, block)
        field[:, columns] = jnp.where(lane < wet[r], raw[:, columns], 0.0).astype(field.dtype)
    copies[-1].wait()


def blended(a, b, early, late):
    mixed = early * a.astype(jnp.float32) + late * b.astype(jnp.float32)
    return mixed.astype(a.dtype).T


def make_table(col, count, _a, _b, _c, _d, table):
    row_blocks, slots = col.shape
    pairs = row_blocks * slots
    halos = halo_places(row_blocks)
    unused = row_blocks + DIRECTIONS
    seconds, others = jnp.int32(0), jnp.int32(0)

    def append(length, first, entry):
        for n, value in enumerate(entry):
            table[(first + n) * pairs + 2 + length] = value

    for r in range(row_blocks):
        known = []
        for k in range(slots):
            slot = col[r, k]
            used = k < count[r]
            aside = unused + 1 + k
            again, rest, later = jnp.bool_(False), jnp.int32(aside), jnp.bool_(False)
            for slot_before, again_before, rest_before in known:
                same = slot_before == slot
                again = again | same
                later = later | (same & again_before)
                rest = jnp.where(same & again_before, rest_before, rest)
            again, later = again & used, later & used
            known.append((slot, again, rest))
            target = place_of(slot, row_blocks, halos)
            table[r * slots + k] = jnp.where(used, jnp.where(again, aside, target), unused)
            entry = (jnp.int32(r), jnp.int32(aside), target)
            append(seconds, 1, entry)
            append(others, 4, (*entry, rest))
            seconds = seconds + (again & ~later).astype(jnp.int32)
            others = others + later.astype(jnp.int32)
    table[pairs] = seconds
    table[pairs + 1] = others
    for n in range(GROUP - 1):
        append(seconds + n, 1, (jnp.int32(0), jnp.int32(unused), jnp.int32(unused)))


def add_repeats(table, dense, pairs, block):
    size = block // PARTS
    parts = range(0, block, size)

    def entry(first, length, e):
        row, *places = [table[(first + n) * pairs + 2 + e] for n in range(length)]
        columns = pl.ds(pl.multiple_of(row * block, block), block)
        return [[(pl.ds(pl.multiple_of(p * block + part, size), size), columns) for p in places] for part in parts]

    def added(*places):
        total = dense[places[0]].astype(jnp.float32)
        for place in places[1:]:
            total = total + dense[place].astype(jnp.float32)
        rounded = total.astype(dense.dtype)
        return rounded, (total - rounded.astype(jnp.float32)).astype(dense.dtype)

    def group(g, carry):
        for entries in zip(*[entry(1, 3, g * GROUP + n) for n in range(GROUP)]):
            sums = [added(target, aside) for aside, target in entries]
            for (aside, target), (rounded, rest) in zip(entries, sums):
                dense[target] = rounded
                dense[aside] = rest
        return carry

    def one(e, carry):
        for aside, target, kept in entry(4, 4, e):
            rounded, rest = added(target, aside, kept)
            dense[target] = rounded
            dense[kept] = rest
        return carry

    lax.fori_loop(0, (table[pairs] + GROUP - 1) // GROUP, group, 0)
    lax.fori_loop(0, table[pairs + 1], one, 0)


def month_weights(day, step):
    now = day[step]
    return (DAYS - now).astype(jnp.float32) * (1.0 / DAYS), now.astype(jnp.float32) * (1.0 / DAYS)


def lay_out(a, b, weights, table, dense, rows):
    slots, block = a.shape[1:3]
    for r in rows:
        for k in range(slots):
            place = pl.ds(pl.multiple_of(table[r * slots + k] * block, block), block)
            dense[place, pl.ds(r * block, block)] = blended(a[r, k], b[r, k], *weights)


def ready_kernel(apply, *refs):
    refs = list(refs)
    explicit, more = apply % 2 == 0, apply + 1 < 2 * STEPS
    day, table, field, a, b, dense = [refs.pop(0) for _ in range(6)]
    next_a, next_b, _ = [refs.pop(0) for _ in range(3)] if more else (None, None, None)
    forcing = refs.pop(0) if explicit else None
    dense, partial = refs[:2]
    row_blocks, slots, block, _ = a.shape
    done, ahead = [row_blocks * share // 8 for share in (AHEAD[apply], AHEAD[apply + 1])]
    lay_out(a, b, month_weights(day, apply // 2), table, dense, range(done, row_blocks))
    add_repeats(table, dense, row_blocks * slots, block)
    total = jnp.dot(field[...], dense[pl.ds(0, field.shape[1]), :], preferred_element_type=jnp.float32)
    partial[...] = total + forcing[...] if explicit else total
    if more:
        lay_out(next_a, next_b, month_weights(day, (apply + 1) // 2), table, refs[2], range(ahead))


def finish_kernel(last, wet, send, partial, dense, in_0, in_1, in_2, in_3, out, *refs):
    tracers, points = partial.shape
    block = in_0.shape[1]
    row_blocks = points // block
    halo = jnp.concatenate([h[...] for h in (in_0, in_1, in_2, in_3)], 1)
    total = partial[...] + jnp.dot(
        halo, dense[pl.ds(points, DIRECTIONS * block), :], preferred_element_type=jnp.float32
    )
    lane = lax.broadcasted_iota(jnp.int32, (tracers, block), 1)
    target = refs[0] if last else out
    for r in range(row_blocks):
        columns = slice(r * block, (r + 1) * block)
        target[:, columns] = jnp.where(lane < wet[r], total[:, columns], 0.0).astype(target.dtype)
    if last:
        copy = pltpu.make_async_copy(target, out, refs[1])
        copy.start()
        copy.wait()
        return
    for n, outgoing in enumerate(refs):
        row = send[direction_of(n)]
        outgoing[...] = out[:, pl.ds(pl.multiple_of(row * block, block), block)]


def on_device(swaps, tracer, source, exp_a, exp_b, imp_a, imp_b, col_index, block_count, send_list, wet_rows, month_day):
    tracers, points = tracer.shape
    row_blocks, slots = col_index.shape
    block = points // row_blocks
    half, full, whole = jnp.bfloat16, jnp.float32, jnp.int32
    hbm = pl.BlockSpec(memory_space=pltpu.HBM)
    vmem = pl.BlockSpec(memory_space=pltpu.VMEM)
    smem = pl.BlockSpec(memory_space=pltpu.SMEM)
    params = pltpu.CompilerParams(vmem_limit_bytes=32 * 1024 * 1024)
    shape = jax.ShapeDtypeStruct
    piece = shape((tracers, block), half)
    field_shape = shape((tracers, points), half)
    partial_shape = shape((tracers, points), full)
    dense_shape = shape(((row_blocks + DIRECTIONS + 1 + slots) * block, points), half)
    dma = pltpu.SemaphoreType.DMA

    def stay(*arrays):
        return [pltpu.with_memory_space_constraint(x, pltpu.HBM) for x in arrays]

    indices = [wet_rows, send_list.reshape(DIRECTIONS), col_index, block_count, month_day]
    *outgoing, field, dense, later, forcing, wet, send, col, count, day = pl.pallas_call(
        prologue_kernel,
        out_shape=[piece] * DIRECTIONS
        + [field_shape, dense_shape, dense_shape, partial_shape]
        + [pltpu.SMEM(x.shape, whole) for x in indices],
        in_specs=[hbm] * 7,
        out_specs=[vmem] * (DIRECTIONS + 4) + [smem] * 5,
        scratch_shapes=[pltpu.VMEM((tracers, points), full), dma((7,))],
        compiler_params=params,
        name="prologue",
    )(*stay(tracer, *indices, source))

    table = pl.pallas_call(
        make_table,
        out_shape=pltpu.SMEM((8 * row_blocks * slots + 2,), whole),
        in_specs=[smem] * 2 + [hbm] * 4,
        out_specs=smem,
        compiler_params=params,
        name="make_table",
    )(col, count, *stay(exp_a, exp_b, imp_a, imp_b))

    def ready(apply, field, dense, later):
        explicit, more = apply % 2 == 0, apply + 1 < 2 * STEPS
        mine, other = ((exp_a, exp_b), (imp_a, imp_b))[:: 1 if explicit else -1]
        operands = [day, table, field, *mine, dense]
        aliases = {5: 0}
        if more:
            operands += [*other, later]
            aliases[8] = 2
        if explicit:
            operands.append(forcing)
        return pl.pallas_call(
            functools.partial(ready_kernel, apply),
            out_shape=[dense_shape, partial_shape] + [dense_shape] * more,
            in_specs=[smem] * 2 + [vmem] * (len(operands) - 2),
            out_specs=[vmem] * (2 + more),
            input_output_aliases=aliases,
            compiler_params=params,
            name="ready",
        )(*operands)

    def finish(last, partial, dense, halos):
        return pl.pallas_call(
            functools.partial(finish_kernel, last),
            out_shape=[partial_shape] if last else [field_shape] + [piece] * DIRECTIONS,
            in_specs=[smem] * 2 + [vmem] * (2 + DIRECTIONS),
            out_specs=[hbm] if last else [vmem] * (1 + DIRECTIONS),
            scratch_shapes=[pltpu.VMEM((tracers, points), full), dma(())] if last else [],
            compiler_params=params,
            name="finish",
        )(wet, send, partial, dense, *halos)

    for apply in range(2 * STEPS):
        halos = [lax.ppermute(p, ("groups", "rows"), s) for p, s in zip(outgoing, swaps)]
        dense, partial, *begun = ready(apply, field, dense, later)
        field, *outgoing = finish(apply + 1 == 2 * STEPS, partial, dense, halos)
        dense, later = begun[0] if begun else None, dense
    return field


def solution(mesh):
    count, groups = mesh.shape["rows"], mesh.shape["groups"]
    swaps = [swap_pairs(count, groups, stride, parity) for stride, parity in SWAPS]
    wide = P("groups", "rows")
    rows = P("rows")
    return jax.shard_map(
        functools.partial(on_device, swaps),
        mesh=mesh,
        in_specs=(wide, wide, rows, rows, rows, rows, rows, rows, rows, rows, P()),
        out_specs=wide,
        check_vma=False,
    )
```
